512 devices in a mesh: chan: 8 (over x, core), tm: 64 (over z, y).
Axes of the slice: x: 4, y: 8, z: 8, core: 2. Of those that a mesh axis runs over, the one named last changes fastest.
Arguments:
- traces: float32 [64, 512, 6144], P('tm', 'chan')
- channel_map: int32 [512], P('chan'), may hold values from 0 to 511, as said below
- pair_blocks: int32 [32, 2], replicated, may hold values from 0 to 31, as said below
- pair_count: int32 [8], replicated, may hold values from 1 to 1024, as said below
Outputs:
- correlations: float32 [8192, 4096], P(('chan', 'tm'))
The draws below stay inside these ranges and needn't reach their ends.
Inputs may be any that keep to these rules, and one draw needn't show every extreme that they name: `channel_map`: entries 64 * d to 64 * d + 63 are an ordering of those same numbers. `pair_blocks`: in every row the first block is at most the second, and the second at most the first plus 4. `pair_count`: some owner has all its pairs live.
All inputs are finite; a program needn't handle non-finite values.
Results may differ from the reference program's by a relative error of at most 0.0017.
Values may be sent and summed in bfloat16 or wider, within the bound.
A program may use at most 64 MiB of HBM per device.

```python
import math
import jax
import jax.numpy as jnp
from jax import lax

CH_DEV = 64
BLOCK_CHANNELS = 16
OWNER_SLOTS = 4
SEG = 6144
TRANSFORM_LENGTH = 16384
BAND_FIRST_BIN = 80
BAND_BINS = 512
LAGS = 4096
TOTAL_CHANNELS = 512
MINUTE_WINDOWS = 64
NBLK = 32
REACH = 4


def draw_traces(key, part):
    key = jax.random.fold_in(key, 11)
    random_key_list = jax.random.split(key, 5)
    full_shape = (MINUTE_WINDOWS, TOTAL_CHANNELS, SEG)
    signal = jax.random.normal(random_key_list[0], full_shape, jnp.float32)
    spread = jnp.exp(jax.random.uniform(random_key_list[1], (MINUTE_WINDOWS, TOTAL_CHANNELS, 1), jnp.float32, 0.0, math.log(10.0)))
    sample_ids = jnp.arange(SEG, dtype=jnp.int32)
    tone_frequency_bins = jax.random.randint(random_key_list[2], (MINUTE_WINDOWS, TOTAL_CHANNELS, 4), BAND_FIRST_BIN, BAND_FIRST_BIN + BAND_BINS)
    tone_amp = jnp.exp(jax.random.uniform(random_key_list[3], (MINUTE_WINDOWS, TOTAL_CHANNELS, 4), jnp.float32, math.log(0.05), math.log(0.5)))
    tone_phase = jax.random.uniform(random_key_list[4], (MINUTE_WINDOWS, TOTAL_CHANNELS, 4), jnp.float32, 0.0, 2.0 * math.pi)
    for tone_idx in range(4):
        angles = jnp.mod(tone_frequency_bins[:, :, tone_idx:tone_idx + 1] * sample_ids, TRANSFORM_LENGTH).astype(jnp.float32) * (2.0 * math.pi / TRANSFORM_LENGTH)
        signal = signal + tone_amp[:, :, tone_idx:tone_idx + 1] * jnp.cos(angles + tone_phase[:, :, tone_idx:tone_idx + 1])
    return signal * spread


def draw_channel_map(key, part):
    key = jax.random.fold_in(key, 23)
    owner_total = TOTAL_CHANNELS // CH_DEV
    random_key_list = jax.random.split(key, owner_total)
    orders = jax.vmap(lambda one_key: jax.random.permutation(one_key, CH_DEV))(random_key_list)
    orders = orders.astype(jnp.int32) + (jnp.arange(owner_total, dtype=jnp.int32) * CH_DEV)[:, None]
    return orders.reshape(-1).astype(jnp.int32)


def draw_pair_blocks(key, part):
    key = jax.random.fold_in(key, 37)
    random_key_list = jax.random.split(key, 2)
    row_total = TOTAL_CHANNELS // CH_DEV * OWNER_SLOTS
    block_first = jax.random.randint(random_key_list[0], (row_total,), 0, NBLK)
    block_gap = jax.random.randint(random_key_list[1], (row_total,), 0, REACH + 1)
    block_second = jnp.minimum(block_first + block_gap, NBLK - 1)
    block_first = block_first.at[0].set(0).at[1].set(NBLK - 1)
    block_second = block_second.at[0].set(REACH).at[1].set(NBLK - 1)
    return jnp.stack([block_first, block_second], axis=1).astype(jnp.int32)


def draw_pair_count(key, part):
    key = jax.random.fold_in(key, 41)
    random_key_list = jax.random.split(key, 2)
    owner_total = TOTAL_CHANNELS // CH_DEV
    most_rows = OWNER_SLOTS * BLOCK_CHANNELS * BLOCK_CHANNELS
    counts = jax.random.randint(random_key_list[0], (owner_total,), 1, most_rows + 1)
    fullest = jax.random.randint(random_key_list[1], (), 0, owner_total)
    return counts.at[fullest].set(most_rows).astype(jnp.int32)


def setup_inputs(seed: int = 0) -> dict:
    key_list = jax.random.split(jax.random.key(seed), 5)
    traces = draw_traces(jax.random.fold_in(key_list[4], 71), 0)
    channel_map = draw_channel_map(jax.random.fold_in(key_list[4], 71), 0)
    pair_blocks = draw_pair_blocks(jax.random.fold_in(key_list[4], 71), 0)
    pair_count = draw_pair_count(jax.random.fold_in(key_list[4], 71), 0)
    return {"traces": traces, "channel_map": channel_map, "pair_blocks": pair_blocks, "pair_count": pair_count}


def whiten_window(minute_window):
    window_spectrum = jnp.fft.rfft(minute_window, n=TRANSFORM_LENGTH, axis=-1)[:, BAND_FIRST_BIN:BAND_FIRST_BIN + BAND_BINS]
    real_part = jnp.real(window_spectrum)
    imag_part = jnp.imag(window_spectrum)
    power = real_part * real_part + imag_part * imag_part
    band_level = lax.optimization_barrier(jnp.mean(power, axis=1, keepdims=True))
    inverse = 1.0 / jnp.sqrt(power + band_level + 1e-06)
    return jnp.concatenate([real_part * inverse, imag_part * inverse], axis=1).astype(jnp.bfloat16)

def cross_sum(first_part, second_part):
    return jnp.einsum('wpif,wpjf->pijf', first_part, second_part, precision=lax.Precision.HIGHEST)

def reference(traces, channel_map, pair_blocks, pair_count):
    whitened = lax.map(whiten_window, traces)
    fibre_rows = jnp.take(whitened, channel_map, axis=1)
    offsets = jnp.arange(BLOCK_CHANNELS, dtype=jnp.int32)
    owner_total = pair_count.shape[0]
    lag_index = jnp.mod(jnp.arange(LAGS, dtype=jnp.int32) - LAGS // 2, TRANSFORM_LENGTH).astype(jnp.int32)
    local_rows = jnp.arange(OWNER_SLOTS * BLOCK_CHANNELS * BLOCK_CHANNELS, dtype=jnp.int32)

    def one_owner(owner_idx):
        owned_pairs = lax.dynamic_slice_in_dim(pair_blocks, owner_idx * OWNER_SLOTS, OWNER_SLOTS, 0)
        rows_first = (owned_pairs[:, 0:1] * BLOCK_CHANNELS + offsets[None, :]).reshape(-1)
        rows_second = (owned_pairs[:, 1:2] * BLOCK_CHANNELS + offsets[None, :]).reshape(-1)
        block_first = jnp.take(fibre_rows, rows_first, axis=1).astype(jnp.float32).reshape(MINUTE_WINDOWS, OWNER_SLOTS, BLOCK_CHANNELS, 2 * BAND_BINS)
        block_second = jnp.take(fibre_rows, rows_second, axis=1).astype(jnp.float32).reshape(MINUTE_WINDOWS, OWNER_SLOTS, BLOCK_CHANNELS, 2 * BAND_BINS)
        left_re = block_first[..., :BAND_BINS]
        left_im = block_first[..., BAND_BINS:]
        right_re = block_second[..., :BAND_BINS]
        right_im = block_second[..., BAND_BINS:]
        stack_norm = 1.0 / math.sqrt(MINUTE_WINDOWS)
        real_sum = (cross_sum(left_re, right_re) + cross_sum(left_im, right_im)) * stack_norm
        imag_sum = (cross_sum(left_im, right_re) - cross_sum(left_re, right_im)) * stack_norm
        window_spectrum = lax.complex(real_sum, imag_sum).reshape(OWNER_SLOTS * BLOCK_CHANNELS * BLOCK_CHANNELS, BAND_BINS)
        zero_padded = jnp.zeros((OWNER_SLOTS * BLOCK_CHANNELS * BLOCK_CHANNELS, TRANSFORM_LENGTH), window_spectrum.dtype).at[:, BAND_FIRST_BIN:BAND_FIRST_BIN + BAND_BINS].set(window_spectrum)
        series = jnp.fft.ifft(zero_padded, axis=-1) * TRANSFORM_LENGTH
        correlation = jnp.real(jnp.take(series, lag_index, axis=1)) * (1.0 / math.sqrt(BAND_BINS))
        live_mask = (local_rows < pair_count[owner_idx]).astype(jnp.float32)
        return correlation * live_mask[:, None]
    result = lax.map(one_owner, jnp.arange(owner_total, dtype=jnp.int32))
    return result.reshape(-1, LAGS)
```

```python
import math

import jax
import jax.numpy as jnp
import numpy as np
from jax import lax
from jax.sharding import PartitionSpec as P

BLOCK_CHANNELS = 16
TRANSFORM_LENGTH = 16384
BAND_FIRST_BIN = 80
BAND_BINS = 512
LAGS = 4096
FIRST = 512
LAG_FIRST = 256
HIGHEST = lax.Precision.HIGHEST


def phase(products):
    angles = np.mod(products, TRANSFORM_LENGTH) * (2.0 * math.pi / TRANSFORM_LENGTH)
    return np.cos(angles).astype(np.float32), np.sin(angles).astype(np.float32)


def forward_spectrum(window):
    rows, samples = window.shape
    bins = BAND_FIRST_BIN + np.arange(BAND_BINS)
    cos_t, sin_t = phase(np.arange(FIRST)[:, None] * bins[None, :])
    cos_w, sin_w = phase(np.arange(samples // FIRST)[:, None] * FIRST * bins[None, :])
    parts = window.reshape(rows, samples // FIRST, FIRST)
    re = jnp.einsum("cba,ak->bck", parts, cos_t, precision=HIGHEST)
    im = jnp.einsum("cba,ak->bck", parts, -sin_t, precision=HIGHEST)
    cos_w, sin_w = cos_w[:, None, :], sin_w[:, None, :]
    return jnp.sum(re * cos_w + im * sin_w, 0), jnp.sum(im * cos_w - re * sin_w, 0)


def whiten(re, im):
    power = re * re + im * im
    level = jnp.mean(power, axis=1, keepdims=True)
    inverse = 1.0 / jnp.sqrt(power + level + 1e-06)
    return (re * inverse).astype(jnp.bfloat16), (im * inverse).astype(jnp.bfloat16)


def inverse_transform(re, im):
    rows = re.shape[0]
    bins = BAND_FIRST_BIN + np.arange(BAND_BINS)
    far = np.arange(LAGS // LAG_FIRST) * LAG_FIRST - LAGS // 2
    cos_w, sin_w = phase(far[:, None, None] * bins[None, None, :])
    cos_t, sin_t = phase(bins[:, None] * np.arange(LAG_FIRST)[None, :])
    table = np.concatenate([cos_t, -sin_t], axis=0)
    turned = jnp.concatenate([re * cos_w - im * sin_w, re * sin_w + im * cos_w], axis=2)
    out = jnp.einsum("nrk,kl->rnl", turned, table, precision=HIGHEST)
    return out.reshape(rows, LAGS) * (1.0 / math.sqrt(BAND_BINS))


def body(traces, channel_map, pair_blocks, pair_count):
    chan_dev = traces.shape[1]
    chans, windows = lax.axis_size("chan"), lax.axis_size("tm")
    re, im = whiten(*forward_spectrum(traces[0]))
    fibre = jnp.stack([re, im], axis=0)
    fibre = jnp.take(fibre, jnp.mod(channel_map, chan_dev), axis=1)
    fibre = jnp.transpose(fibre.reshape(2, chan_dev, windows, chans), (2, 3, 1, 0))
    fibre = lax.all_to_all(fibre, "tm", 0, 0, tiled=True)
    fibre = jnp.transpose(fibre, (1, 2, 0, 3))
    fibre = lax.all_to_all(fibre, "chan", 0, 0, tiled=True)
    blocks = fibre.reshape(-1, BLOCK_CHANNELS, windows, 2).astype(jnp.float32)
    left = jnp.take(blocks, pair_blocks[:, 0], axis=0)
    right = jnp.take(blocks, pair_blocks[:, 1], axis=0)
    swapped = jnp.stack([right[..., 1], -right[..., 0]], axis=-1)
    both = jnp.stack([right, -swapped], axis=1).reshape(right.shape[0], 2, BLOCK_CHANNELS, -1)
    left = left.reshape(left.shape[0], BLOCK_CHANNELS, -1)
    stacked = jnp.einsum("piw,pcjw->pijc", left, both, precision=HIGHEST) * (1.0 / math.sqrt(windows))
    stacked = stacked.reshape(chans, -1, 2)
    stacked = lax.all_to_all(stacked, "chan", 0, 0, tiled=True)
    stacked = jnp.transpose(stacked.reshape(chans, windows, -1, 2), (1, 0, 2, 3))
    stacked = lax.all_to_all(stacked, "tm", 0, 0, tiled=True)
    stacked = jnp.transpose(stacked.reshape(BAND_BINS, -1, 2), (2, 1, 0))
    rows = stacked.shape[1]
    row_ids = lax.axis_index("tm") * rows + jnp.arange(rows, dtype=jnp.int32)
    live = lax.dynamic_slice_in_dim(pair_count, lax.axis_index("chan"), 1, 0)
    mask = (row_ids < live).astype(jnp.float32)
    return inverse_transform(stacked[0], stacked[1]) * mask[:, None]


def solution(mesh):
    placed = (P("tm", "chan", None), P("chan"), P(), P())
    return jax.shard_map(
        body, mesh=mesh, in_specs=placed, out_specs=P(("chan", "tm"), None), check_vma=False
    )
```

```python
import functools
import math

import jax
import jax.numpy as jnp
import numpy as np
from jax import lax
from jax.experimental import pallas as pl
from jax.experimental.pallas import tpu as pltpu
from jax.sharding import PartitionSpec as P

BLOCK = 16
SLOTS = 4
TRANSFORM_LENGTH = 16384
BAND_FIRST_BIN = 80
BINS = 512
LAGS = 4096
NEAR = 512
LAG_NEAR = 256
LANES = 128
MESH = pl.DeviceIdType.MESH
F32 = jnp.float32
BF16 = jnp.bfloat16


def phase(products):
    angles = np.mod(products, TRANSFORM_LENGTH) * (2.0 * math.pi / TRANSFORM_LENGTH)
    return np.cos(angles), np.sin(angles)


def split(table):
    table = table.astype(np.float32)
    high = table.astype(BF16)
    low = (table - high.astype(np.float32)).astype(BF16)
    return np.stack([high, low])


def forward_tables(samples):
    bins = BAND_FIRST_BIN + np.arange(BINS)
    cos, sin = phase(np.arange(NEAR)[:, None] * bins[None, :])
    tiles = BINS // LANES
    table = np.stack([cos.reshape(NEAR, tiles, LANES), -sin.reshape(NEAR, tiles, LANES)], axis=2)
    turn = phase(np.arange(samples // NEAR)[:, None] * NEAR * bins[None, :])
    return split(table.reshape(NEAR, 2 * BINS)), np.stack(turn).astype(np.float32)


def inverse_tables(scale):
    lane = np.arange(BINS)
    order = 8 * (lane % 64) + 4 * (lane // 64 % 2) + lane // 128
    bins = BAND_FIRST_BIN + order
    cos, sin = phase(bins[:, None] * np.arange(LAG_NEAR)[None, :])
    table = np.concatenate([cos, -sin], axis=0) * scale
    far = np.arange(LAGS // LAG_NEAR) * LAG_NEAR - LAGS // 2
    turn = phase(far[:, None] * bins[None, :])
    return split(table), np.stack(turn).astype(np.float32)


def halves(value):
    high = value.astype(BF16)
    return high, (value - high.astype(F32)).astype(BF16)


def zigzag(step):
    return 4 + (step + 1) // 2 * (1 - 2 * (step % 2))


def kernel(
    chans, windows,
    x_hbm, map_hbm, pairs_hbm, count_hbm, fwd_hbm, fturn_hbm, inv_hbm, iturn_hbm,
    out_ref,
    x_ref, map_ref, pairs_ref, count_ref, fwd_ref, fturn_ref, inv_ref, iturn_ref,
    high_ref, low_ref, z_ref, spec_ref,
    g_ref, r1_ref, s_ref, r2_ref, h_ref, sel_ref, pick_ref, m_ref, q_ref, m2_ref, u_ref, lag_h, lag_l,
    load_sem, send_sem, recv_sem,
):
    c, t = lax.axis_index("chan"), lax.axis_index("tm")
    rows, samples = x_ref.shape
    sections = samples // NEAR
    loads = [
        pltpu.make_async_copy(source, target, load_sem.at[k])
        for k, (source, target) in enumerate(
            (
                (x_hbm, x_ref), (fwd_hbm, fwd_ref), (fturn_hbm, fturn_ref), (map_hbm, map_ref),
                (pairs_hbm, pairs_ref), (count_hbm, count_ref), (inv_hbm, inv_ref), (iturn_hbm, iturn_ref),
            )
        )
    ]
    for load in loads:
        load.start()

    def window_peer(step):
        z = lax.rem(t // 8 + zigzag(step // 8), 8)
        y = lax.rem(lax.rem(t, 8) + zigzag(step % 8), 8)
        return z * 8 + y

    barrier = pltpu.get_barrier_semaphore()

    @pl.loop(0, windows - 1)
    def _(step):
        pl.semaphore_signal(barrier, 1, device_id=(c, window_peer(step)), device_id_type=MESH)

    @pl.loop(1, chans)
    def _(step):
        pl.semaphore_signal(barrier, 1, device_id=(lax.rem(c + step, chans), t), device_id_type=MESH)

    loads[0].wait()
    for b in range(sections):
        high, low = halves(x_ref[:, b * NEAR : (b + 1) * NEAR])
        high_ref[b * rows : (b + 1) * rows, :] = high
        low_ref[b * rows : (b + 1) * rows, :] = low
    loads[1].wait()
    loads[2].wait()

    for n in range(BINS // LANES):
        cols = slice(2 * LANES * n, 2 * LANES * (n + 1))
        z_ref[...] = (
            jnp.dot(high_ref[...], fwd_ref[0, :, cols], preferred_element_type=F32)
            + jnp.dot(low_ref[...], fwd_ref[0, :, cols], preferred_element_type=F32)
            + jnp.dot(high_ref[...], fwd_ref[1, :, cols], preferred_element_type=F32)
        )
        lanes = slice(LANES * n, LANES * (n + 1))
        re = jnp.zeros((rows, LANES), F32)
        im = jnp.zeros((rows, LANES), F32)
        for b in range(sections):
            zr = z_ref[b * rows : (b + 1) * rows, :LANES]
            zi = z_ref[b * rows : (b + 1) * rows, LANES:]
            cw = fturn_ref[0, b : b + 1, lanes]
            sw = fturn_ref[1, b : b + 1, lanes]
            re += zr * cw + zi * sw
            im += zi * cw - zr * sw
        spec_ref[:rows, lanes] = re
        spec_ref[rows:, lanes] = im

    re, im = spec_ref[:rows, :], spec_ref[rows:, :]
    power = re * re + im * im
    level = jnp.mean(power, axis=1, keepdims=True)
    inverse = 1.0 / jnp.sqrt(power + level + 1e-06)
    white = jnp.concatenate([re * inverse, im * inverse], axis=0).astype(BF16)

    loads[3].wait()
    place = jnp.bitwise_and(map_ref[...], rows - 1).reshape(1, rows)
    place = jnp.concatenate([place, place + rows], axis=1)
    pick = (lax.broadcasted_iota(jnp.int32, (2 * rows, 2 * rows), 0) == place).astype(F32).astype(BF16)
    g = lax.dot_general(white, pick, (((0,), (0,)), ((), ())), preferred_element_type=F32)
    g_ref[...] = g.reshape(windows, chans, 2 * rows)

    pl.semaphore_wait(barrier, windows + chans - 2)

    def send_window(source, target, k):
        def body(step, carry):
            peer = window_peer(step)
            pltpu.make_async_remote_copy(
                src_ref=source.at[peer], dst_ref=target.at[t], send_sem=send_sem.at[k],
                recv_sem=recv_sem.at[k], device_id=(c, peer), device_id_type=MESH,
            ).start()
            return carry

        lax.fori_loop(0, windows - 1, body, 0, unroll=7)
        target[t] = source[t]

    def arrived(target, k):
        part = target.at[pl.ds(0, target.shape[0] - 1)]
        pltpu.make_async_copy(part, part, recv_sem.at[k]).wait()

    def sent(source, k):
        part = source.at[pl.ds(0, source.shape[0] - 1)]
        pltpu.make_async_copy(part, part, send_sem.at[k]).wait()

    send_window(g_ref, r1_ref, 0)

    for load in loads[4:]:
        load.wait()
    pairs = pairs_ref.shape[1]
    gap = lax.broadcasted_iota(jnp.int32, (BLOCK, chans * rows), 1) - lax.broadcasted_iota(
        jnp.int32, (BLOCK, chans * rows), 0
    )
    for side in range(2):
        for p in range(pairs):
            hit = gap == pairs_ref[side, p] * BLOCK
            first = (side * pairs + p) * BLOCK
            sel_ref[first : first + BLOCK, :] = hit.astype(F32).astype(BF16)
    arrived(r1_ref, 0)
    for q in range(chans):
        s_ref[q] = r1_ref[:, q, :].astype(BF16)

    @pl.loop(1, chans)
    def _(step):
        peer = lax.rem(c + step, chans)
        pltpu.make_async_remote_copy(
            src_ref=s_ref.at[peer], dst_ref=r2_ref.at[c], send_sem=send_sem.at[1],
            recv_sem=recv_sem.at[1], device_id=(peer, t), device_id_type=MESH,
        ).start()

    r2_ref[c] = s_ref[c]
    arrived(r2_ref, 1)

    for d in range(chans):
        turned = r2_ref[d].astype(F32).T
        re, im = turned[:rows], turned[rows:]
        h_ref[d * rows : (d + 1) * rows, :] = jnp.concatenate([re, im, -im, re], axis=1).astype(BF16)
    pick_ref[...] = jnp.dot(sel_ref[...], h_ref[...], preferred_element_type=F32).astype(BF16)

    wide = SLOTS * BLOCK
    same = (
        lax.broadcasted_iota(jnp.int32, (wide, LANES), 0) // BLOCK
        == lax.broadcasted_iota(jnp.int32, (wide, LANES), 1) // (2 * BLOCK)
    )

    def owner_pairs(owner):
        first = pl.multiple_of(owner * wide, wide)
        left = pick_ref[pl.ds(first, wide), :LANES]
        both = pick_ref[pl.ds(pairs * BLOCK + first, wide), :]
        right = []
        for s in range(SLOTS):
            right += [both[s * BLOCK : (s + 1) * BLOCK, :LANES], both[s * BLOCK : (s + 1) * BLOCK, LANES:]]
        right = jnp.concatenate(right, axis=0)
        cross = lax.dot_general(left, right, (((1,), (1,)), ((), ())), preferred_element_type=F32)
        cross = jnp.where(same, cross, 0.0)
        return sum(cross[s * BLOCK : (s + 1) * BLOCK] for s in range(SLOTS))

    @pl.loop(1, chans)
    def _(step):
        owner = lax.rem(c + step, chans)
        m_ref[owner] = owner_pairs(owner)
        pltpu.make_async_remote_copy(
            src_ref=m_ref.at[owner], dst_ref=q_ref.at[c], send_sem=send_sem.at[2],
            recv_sem=recv_sem.at[2], device_id=(owner, t), device_id_type=MESH,
        ).start()

    q_ref[c] = owner_pairs(c)
    arrived(q_ref, 2)

    block = lax.broadcasted_iota(jnp.int32, (BLOCK, LANES), 1) // (2 * BLOCK)
    for s in range(SLOTS):
        for h in range(2):
            mixed = jnp.zeros((BLOCK, LANES), F32)
            for k in range(4):
                part = q_ref[4 * h + k]
                shift = (k - s) * 2 * BLOCK % LANES
                part = pltpu.roll(part, shift, 1) if shift else part
                mixed = jnp.where(block == k, part, mixed)
            m2_ref[s * BLOCK : (s + 1) * BLOCK, h, :] = mixed
    send_window(m2_ref, u_ref, 3)
    arrived(u_ref, 3)

    turned = jnp.concatenate([u_ref[:, 0, :], u_ref[:, 1, :]], axis=0).T
    row_ids = t * BLOCK + lax.broadcasted_iota(jnp.int32, (BLOCK, 1), 0)
    live = (row_ids < count_ref[c]).astype(F32)
    re = jnp.concatenate([turned[32 * k : 32 * k + 16] for k in range(4)], axis=1) * live
    im = jnp.concatenate([turned[32 * k + 16 : 32 * k + 32] for k in range(4)], axis=1) * live
    for n in range(LAGS // LAG_NEAR):
        cw, sw = iturn_ref[0, n : n + 1, :], iturn_ref[1, n : n + 1, :]
        place = slice(n * BLOCK, (n + 1) * BLOCK)
        high, low = halves(re * cw - im * sw)
        lag_h[place, :BINS] = high
        lag_l[place, :BINS] = low
        high, low = halves(re * sw + im * cw)
        lag_h[place, BINS:] = high
        lag_l[place, BINS:] = low
    lags = (
        jnp.dot(lag_h[...], inv_ref[0], preferred_element_type=F32)
        + jnp.dot(lag_l[...], inv_ref[0], preferred_element_type=F32)
        + jnp.dot(lag_h[...], inv_ref[1], preferred_element_type=F32)
    )
    for n in range(LAGS // LAG_NEAR):
        out_ref[:, n * LAG_NEAR : (n + 1) * LAG_NEAR] = lags[n * BLOCK : (n + 1) * BLOCK]
    sent(g_ref, 0)
    sent(s_ref, 1)
    sent(m_ref, 2)
    sent(m2_ref, 3)


def solution(mesh):
    chans, windows = mesh.shape["chan"], mesh.shape["tm"]

    def body(traces, channel_map, pair_blocks, pair_count):
        _, rows, samples = traces.shape
        fwd, fturn = forward_tables(samples)
        inv, iturn = inverse_tables(1.0 / math.sqrt(windows * BINS))
        sections, far = samples // NEAR, LAGS // LAG_NEAR
        vmem = pl.BlockSpec(memory_space=pltpu.VMEM)
        hbm = pl.BlockSpec(memory_space=pl.ANY)
        return pl.pallas_call(
            functools.partial(kernel, chans, windows),
            out_shape=jax.ShapeDtypeStruct((BLOCK, LAGS), F32),
            in_specs=[hbm] * 8,
            out_specs=vmem,
            scratch_shapes=[
                pltpu.VMEM((rows, samples), F32),
                pltpu.VMEM(channel_map.shape, jnp.int32),
                pltpu.SMEM(pair_blocks.shape[::-1], jnp.int32),
                pltpu.SMEM(pair_count.shape, jnp.int32),
                pltpu.VMEM(fwd.shape, BF16),
                pltpu.VMEM(fturn.shape, F32),
                pltpu.VMEM(inv.shape, BF16),
                pltpu.VMEM(iturn.shape, F32),
                pltpu.VMEM((sections * rows, NEAR), BF16),
                pltpu.VMEM((sections * rows, NEAR), BF16),
                pltpu.VMEM((sections * rows, 2 * LANES), F32),
                pltpu.VMEM((2 * rows, BINS), F32),
                pltpu.VMEM((windows, chans, 2 * rows), F32),
                pltpu.VMEM((windows, chans, 2 * rows), F32),
                pltpu.VMEM((chans, windows, 2 * rows), BF16),
                pltpu.VMEM((chans, windows, 2 * rows), BF16),
                pltpu.VMEM((chans * rows, 4 * windows), BF16),
                pltpu.VMEM((2 * pair_blocks.shape[0] * BLOCK, chans * rows), BF16),
                pltpu.VMEM((2 * pair_blocks.shape[0] * BLOCK, 4 * windows), BF16),
                pltpu.VMEM((chans, BLOCK, LANES), F32),
                pltpu.VMEM((chans, BLOCK, LANES), F32),
                pltpu.VMEM((windows, 2, LANES), F32),
                pltpu.VMEM((windows, 2, LANES), F32),
                pltpu.VMEM((far * BLOCK, 2 * BINS), BF16),
                pltpu.VMEM((far * BLOCK, 2 * BINS), BF16),
                pltpu.SemaphoreType.DMA((8,)),
                pltpu.SemaphoreType.DMA((4,)),
                pltpu.SemaphoreType.DMA((4,)),
            ],
            compiler_params=pltpu.CompilerParams(
                collective_id=0, has_side_effects=True, vmem_limit_bytes=63 << 20
            ),
            name="correlate",
        )(traces[0], channel_map, pair_blocks.T, pair_count, fwd, fturn, inv, iturn)

    placed = (P("tm", "chan", None), P("chan"), P(), P())
    return jax.shard_map(
        body, mesh=mesh, in_specs=placed, out_specs=P(("chan", "tm"), None), check_vma=False
    )
```

```python
import functools
import math

import jax
import jax.numpy as jnp
import numpy as np
from jax import lax
from jax.experimental import pallas as pl
from jax.experimental.pallas import tpu as pltpu
from jax.sharding import PartitionSpec as P

BLOCK = 16
SLOTS = 4
TRANSFORM_LENGTH = 16384
BAND_FIRST_BIN = 80
BINS = 512
LAGS = 4096
NEAR = 512
LAG_NEAR = 512
LANES = 128
MESH = pl.DeviceIdType.MESH
F32 = jnp.float32
BF16 = jnp.bfloat16


def phase(products, length=TRANSFORM_LENGTH):
    angles = np.mod(products, length) * (2.0 * math.pi / length)
    return np.cos(angles), np.sin(angles)


def split(table):
    table = table.astype(np.float32)
    high = table.astype(BF16)
    low = (table - high.astype(np.float32)).astype(BF16)
    return np.stack([high, low])


def forward_tables(samples):
    bins = BAND_FIRST_BIN + np.arange(BINS)
    offset = 2 * np.arange(NEAR // 2) + 1
    cos, sin = phase(offset[:, None] * bins[None, :], 2 * TRANSFORM_LENGTH)
    centre = 2 * NEAR * np.arange(samples // NEAR) + NEAR - 1
    turn = phase(centre[:, None] * bins[None, :], 2 * TRANSFORM_LENGTH)
    return split(np.stack([cos, -sin])), np.stack(turn).astype(np.float32)


def inverse_tables(scale):
    lane = np.arange(BINS)
    order = 8 * (lane % 64) + 4 * (lane // 64 % 2) + lane // 128
    bins = BAND_FIRST_BIN + order
    cos, sin = phase(bins[:, None] * np.arange(LAG_NEAR)[None, :])
    table = np.concatenate([cos, -sin], axis=0) * scale
    far = np.arange(LAGS // LAG_NEAR) * LAG_NEAR - LAGS // 2
    turn = phase(far[:, None] * bins[None, :])
    return split(table), np.stack(turn).astype(np.float32)


def halves(value):
    high = value.astype(BF16)
    return high, (value - high.astype(F32)).astype(BF16)


def zigzag(step):
    return 4 + (step + 1) // 2 * (1 - 2 * (step % 2))


def kernel(
    chans, windows,
    x_hbm, map_hbm, pairs_hbm, count_hbm, fwd_hbm, fturn_hbm, inv_hbm, iturn_hbm,
    out_ref,
    x_ref, map_ref, pairs_ref, count_ref, fwd_ref, fturn_ref, inv_ref, iturn_ref,
    even_h, even_l, odd_h, odd_l, zr_ref, zi_ref, spec_ref,
    g_ref, r1_ref, wide_ref, s_ref, r2_ref, h_ref, sel_ref, m_ref, q_ref, m2_ref, u_ref, lag_h, lag_l,
    load_sem, send_sem, recv_sem,
):
    c, t = lax.axis_index("chan"), lax.axis_index("tm")
    rows, samples = x_ref.shape
    sections = samples // NEAR
    ends = [
        (x_hbm, x_ref), (fwd_hbm, fwd_ref), (fturn_hbm, fturn_ref), (map_hbm, map_ref),
        (pairs_hbm, pairs_ref), (count_hbm, count_ref), (iturn_hbm, iturn_ref), (inv_hbm, inv_ref),
    ]
    loads = [
        pltpu.make_async_copy(source, target, load_sem.at[k]) for k, (source, target) in enumerate(ends)
    ]
    def window_peer(step):
        z = lax.rem(t // 8 + zigzag(step // 8), 8)
        y = lax.rem(lax.rem(t, 8) + zigzag(step % 8), 8)
        return z * 8 + y

    barrier = pltpu.get_barrier_semaphore()

    def greet(step):
        pl.semaphore_signal(barrier, 1, device_id=(c, window_peer(step)), device_id_type=MESH)

    pl.loop(0, windows // 2)(greet)
    for load in loads[:6]:
        load.start()
    pl.loop(windows // 2, windows - 1)(greet)

    @pl.loop(1, chans)
    def _(step):
        pl.semaphore_signal(barrier, 1, device_id=(lax.rem(c + step, chans), t), device_id_type=MESH)

    half = NEAR // 2
    mirror = (
        lax.broadcasted_iota(jnp.int32, (half, half), 0) + lax.broadcasted_iota(jnp.int32, (half, half), 1)
        == half - 1
    ).astype(F32).astype(BF16)
    loads[0].wait()
    for b in range(sections):
        place = slice(b * rows, (b + 1) * rows)
        even_h[place, :], even_l[place, :] = halves(x_ref[:, b * NEAR : b * NEAR + half])
    back = jnp.dot(even_h[...], mirror, preferred_element_type=F32) + jnp.dot(
        even_l[...], mirror, preferred_element_type=F32
    )
    for b in range(sections):
        place = slice(b * rows, (b + 1) * rows)
        ahead = x_ref[:, b * NEAR + half : (b + 1) * NEAR]
        even_h[place, :], even_l[place, :] = halves(ahead + back[place])
        odd_h[place, :], odd_l[place, :] = halves(ahead - back[place])
    loads[1].wait()
    loads[2].wait()
    for load in loads[6:]:
        load.start()

    def product(high, low, part, lanes):
        return (
            jnp.dot(high[...], fwd_ref[0, part, :, lanes], preferred_element_type=F32)
            + jnp.dot(low[...], fwd_ref[0, part, :, lanes], preferred_element_type=F32)
            + jnp.dot(high[...], fwd_ref[1, part, :, lanes], preferred_element_type=F32)
        )

    for n in range(BINS // half):
        lanes = slice(half * n, half * (n + 1))
        zr_ref[...] = product(even_h, even_l, 0, lanes)
        zi_ref[...] = product(odd_h, odd_l, 1, lanes)
        re = jnp.zeros((rows, half), F32)
        im = jnp.zeros((rows, half), F32)
        for b in range(sections):
            zr = zr_ref[b * rows : (b + 1) * rows, :]
            zi = zi_ref[b * rows : (b + 1) * rows, :]
            cw = fturn_ref[0, b : b + 1, lanes]
            sw = fturn_ref[1, b : b + 1, lanes]
            re += zr * cw + zi * sw
            im += zi * cw - zr * sw
        spec_ref[:rows, lanes] = re
        spec_ref[rows:, lanes] = im

    re, im = spec_ref[:rows, :], spec_ref[rows:, :]
    power = re * re + im * im
    level = jnp.mean(power, axis=1, keepdims=True)
    inverse = 1.0 / jnp.sqrt(power + level + 1e-06)
    white = jnp.concatenate([re * inverse, im * inverse], axis=0).astype(BF16)

    loads[3].wait()
    place = jnp.bitwise_and(map_ref[...], rows - 1).reshape(1, rows)
    place = jnp.concatenate([place, place + rows], axis=1)
    pick = (lax.broadcasted_iota(jnp.int32, (2 * rows, 2 * rows), 0) == place).astype(F32).astype(BF16)
    g = lax.dot_general(white, pick, (((0,), (0,)), ((), ())), preferred_element_type=F32)
    g_ref[...] = g.reshape(windows, chans, 2 * rows).astype(BF16)

    pl.semaphore_wait(barrier, windows + chans - 2)

    def send_window(source, target, k):
        def body(step, carry):
            peer = window_peer(step)
            pltpu.make_async_remote_copy(
                src_ref=source.at[peer], dst_ref=target.at[t], send_sem=send_sem.at[k],
                recv_sem=recv_sem.at[k], device_id=(c, peer), device_id_type=MESH,
            ).start()
            return carry

        lax.fori_loop(0, windows - 1, body, 0, unroll=7)
        target[t] = source[t]

    def arrived(ref, k):
        rest = ref.at[pl.ds(0, ref.shape[0] - 1)]
        pltpu.make_async_copy(rest, rest, recv_sem.at[k]).wait()

    def sent(ref, k):
        rest = ref.at[pl.ds(0, ref.shape[0] - 1)]
        pltpu.make_async_copy(rest, rest, send_sem.at[k]).wait()

    send_window(g_ref, r1_ref, 0)

    for load in loads[4:]:
        load.wait()
    gap = lax.broadcasted_iota(jnp.int32, (BLOCK, chans * rows), 1) - lax.broadcasted_iota(
        jnp.int32, (BLOCK, chans * rows), 0
    )
    wide = SLOTS * BLOCK
    owners = [lax.rem(c + zigzag(step) % chans, chans) for step in range(chans)]
    for step in range(chans):
        for side in range(2):
            for s in range(SLOTS):
                hit = gap == pairs_ref[side, owners[step] * SLOTS + s] * BLOCK
                first = (step * 2 + side) * wide + s * BLOCK
                sel_ref[first : first + BLOCK, :] = hit.astype(F32).astype(BF16)
    arrived(r1_ref, 0)
    wide_ref[...] = r1_ref[...].astype(F32)
    for q in range(chans):
        s_ref[q] = wide_ref[:, q, :].astype(BF16)

    @pl.loop(0, chans - 1)
    def _(step):
        peer = lax.rem(c + zigzag(step), chans)
        pltpu.make_async_remote_copy(
            src_ref=s_ref.at[peer], dst_ref=r2_ref.at[c], send_sem=send_sem.at[1],
            recv_sem=recv_sem.at[1], device_id=(peer, t), device_id_type=MESH,
        ).start()

    r2_ref[c] = s_ref[c]
    arrived(r2_ref, 1)

    for d in range(0, chans, 2):
        one = r2_ref[d].astype(F32)
        two = r2_ref[d + 1].astype(F32)
        first = lax.broadcasted_iota(jnp.int32, one.shape, 1) < rows
        re = jnp.where(first, one, pltpu.roll(two, rows, 1))
        im = jnp.where(first, pltpu.roll(one, rows, 1), two)
        value = jnp.concatenate([re, im, -im, re], axis=0)
        h_ref[:, d * rows : (d + 2) * rows] = value.astype(BF16)
    pick = lax.dot_general(
        sel_ref[...], h_ref[...], (((1,), (1,)), ((), ())), preferred_element_type=F32
    ).astype(BF16)

    same = (
        lax.broadcasted_iota(jnp.int32, (wide, LANES), 0) // BLOCK
        == lax.broadcasted_iota(jnp.int32, (wide, LANES), 1) // (2 * BLOCK)
    )

    def owner_pairs(step):
        left = pick[2 * step * wide : (2 * step + 1) * wide, :LANES]
        both = pick[(2 * step + 1) * wide : (2 * step + 2) * wide]
        right = []
        for s in range(SLOTS):
            right += [both[s * BLOCK : (s + 1) * BLOCK, :LANES], both[s * BLOCK : (s + 1) * BLOCK, LANES:]]
        right = jnp.concatenate(right, axis=0)
        cross = lax.dot_general(left, right, (((1,), (1,)), ((), ())), preferred_element_type=F32)
        cross = jnp.where(same, cross, 0.0)
        return sum(cross[s * BLOCK : (s + 1) * BLOCK] for s in range(SLOTS))

    for step in range(chans - 1):
        m_ref[step] = owner_pairs(step)
        pltpu.make_async_remote_copy(
            src_ref=m_ref.at[step], dst_ref=q_ref.at[c], send_sem=send_sem.at[2],
            recv_sem=recv_sem.at[2], device_id=(owners[step], t), device_id_type=MESH,
        ).start()
    q_ref[c] = owner_pairs(chans - 1)
    arrived(q_ref, 2)

    block = lax.broadcasted_iota(jnp.int32, (BLOCK, LANES), 1) // (2 * BLOCK)
    for s in range(SLOTS):
        for h in range(2):
            mixed = jnp.zeros((BLOCK, LANES), F32)
            for k in range(4):
                part = q_ref[4 * h + k]
                shift = (k - s) * 2 * BLOCK % LANES
                part = pltpu.roll(part, shift, 1) if shift else part
                mixed = jnp.where(block == k, part, mixed)
            m2_ref[s * BLOCK : (s + 1) * BLOCK, h, :] = mixed
    send_window(m2_ref, u_ref, 3)
    arrived(u_ref, 3)

    turned = jnp.concatenate([u_ref[:, 0, :], u_ref[:, 1, :]], axis=0).T
    row_ids = t * BLOCK + lax.broadcasted_iota(jnp.int32, (BLOCK, 1), 0)
    live = (row_ids < count_ref[c]).astype(F32)
    re = jnp.concatenate([turned[32 * k : 32 * k + 16] for k in range(4)], axis=1) * live
    im = jnp.concatenate([turned[32 * k + 16 : 32 * k + 32] for k in range(4)], axis=1) * live
    for n in range(LAGS // LAG_NEAR):
        cw, sw = iturn_ref[0, n : n + 1, :], iturn_ref[1, n : n + 1, :]
        place = slice(n * BLOCK, (n + 1) * BLOCK)
        high, low = halves(re * cw - im * sw)
        lag_h[place, :BINS] = high
        lag_l[place, :BINS] = low
        high, low = halves(re * sw + im * cw)
        lag_h[place, BINS:] = high
        lag_l[place, BINS:] = low
    lags = (
        jnp.dot(lag_h[...], inv_ref[0], preferred_element_type=F32)
        + jnp.dot(lag_l[...], inv_ref[0], preferred_element_type=F32)
        + jnp.dot(lag_h[...], inv_ref[1], preferred_element_type=F32)
    )
    for n in range(LAGS // LAG_NEAR):
        out_ref[:, n * LAG_NEAR : (n + 1) * LAG_NEAR] = lags[n * BLOCK : (n + 1) * BLOCK]
    sent(g_ref, 0)
    sent(s_ref, 1)
    sent(m_ref, 2)
    sent(m2_ref, 3)


def solution(mesh):
    chans, windows = mesh.shape["chan"], mesh.shape["tm"]

    def body(traces, channel_map, pair_blocks, pair_count):
        _, rows, samples = traces.shape
        fwd, fturn = forward_tables(samples)
        inv, iturn = inverse_tables(1.0 / math.sqrt(windows * BINS))
        sections, far = samples // NEAR, LAGS // LAG_NEAR
        vmem = pl.BlockSpec(memory_space=pltpu.VMEM)
        hbm = pl.BlockSpec(memory_space=pltpu.HBM)
        return pl.pallas_call(
            functools.partial(kernel, chans, windows),
            out_shape=pltpu.VMEM((BLOCK, LAGS), F32),
            in_specs=[hbm] * 8,
            out_specs=vmem,
            scratch_shapes=[
                pltpu.VMEM((rows, samples), F32),
                pltpu.VMEM(channel_map.shape, jnp.int32),
                pltpu.SMEM(pair_blocks.shape[::-1], jnp.int32),
                pltpu.SMEM(pair_count.shape, jnp.int32),
                pltpu.VMEM(fwd.shape, BF16),
                pltpu.VMEM(fturn.shape, F32),
                pltpu.VMEM(inv.shape, BF16),
                pltpu.VMEM(iturn.shape, F32),
                pltpu.VMEM((sections * rows, NEAR // 2), BF16),
                pltpu.VMEM((sections * rows, NEAR // 2), BF16),
                pltpu.VMEM((sections * rows, NEAR // 2), BF16),
                pltpu.VMEM((sections * rows, NEAR // 2), BF16),
                pltpu.VMEM((sections * rows, NEAR // 2), F32),
                pltpu.VMEM((sections * rows, NEAR // 2), F32),
                pltpu.VMEM((2 * rows, BINS), F32),
                pltpu.VMEM((windows, chans, 2 * rows), BF16),
                pltpu.VMEM((windows, chans, 2 * rows), BF16),
                pltpu.VMEM((windows, chans, 2 * rows), F32),
                pltpu.VMEM((chans, windows, 2 * rows), BF16),
                pltpu.VMEM((chans, windows, 2 * rows), BF16),
                pltpu.VMEM((4 * windows, chans * rows), BF16),
                pltpu.VMEM((2 * pair_blocks.shape[0] * BLOCK, chans * rows), BF16),
                pltpu.VMEM((chans, BLOCK, LANES), F32),
                pltpu.VMEM((chans, BLOCK, LANES), F32),
                pltpu.VMEM((windows, 2, LANES), F32),
                pltpu.VMEM((windows, 2, LANES), F32),
                pltpu.VMEM((far * BLOCK, 2 * BINS), BF16),
                pltpu.VMEM((far * BLOCK, 2 * BINS), BF16),
                pltpu.SemaphoreType.DMA((8,)),
                pltpu.SemaphoreType.DMA((4,)),
                pltpu.SemaphoreType.DMA((4,)),
            ],
            compiler_params=pltpu.CompilerParams(
                collective_id=0, has_side_effects=True, vmem_limit_bytes=56 << 20
            ),
            name="correlate",
        )(traces[0], channel_map, pair_blocks.T, pair_count, fwd, fturn, inv, iturn)

    placed = (P("tm", "chan", None), P("chan"), P(), P())
    return jax.shard_map(
        body, mesh=mesh, in_specs=placed, out_specs=P(("chan", "tm"), None), check_vma=False
    )
```

```python
import functools
import math

import jax
import jax.numpy as jnp
import numpy as np
from jax import lax
from jax.experimental import pallas as pl
from jax.experimental.pallas import tpu as pltpu
from jax.sharding import PartitionSpec as P

BLOCK = 16
SLOTS = 4
TRANSFORM_LENGTH = 16384
BAND_FIRST_BIN = 80
BINS = 512
LAGS = 4096
NEAR = 512
LAG_NEAR = 512
LANES = 128
MESH = pl.DeviceIdType.MESH
F32 = jnp.float32
BF16 = jnp.bfloat16


def phase(products, length=TRANSFORM_LENGTH):
    angles = np.mod(products, length) * (2.0 * math.pi / length)
    return np.cos(angles), np.sin(angles)


def split(table):
    table = table.astype(np.float32)
    high = table.astype(BF16)
    low = (table - high.astype(np.float32)).astype(BF16)
    return np.stack([high, low])


def forward_tables(samples):
    bins = BAND_FIRST_BIN + np.arange(BINS)
    offset = 2 * np.arange(NEAR // 2) + 1
    cos, sin = phase(offset[:, None] * bins[None, :], 2 * TRANSFORM_LENGTH)
    centre = 2 * NEAR * np.arange(samples // NEAR) + NEAR - 1
    turn = phase(centre[:, None] * bins[None, :], 2 * TRANSFORM_LENGTH)
    return split(np.stack([cos, -sin])), np.stack(turn).astype(np.float32)


def inverse_tables(scale):
    lane = np.arange(BINS)
    order = 8 * (lane % 64) + 4 * (lane // 64 % 2) + lane // 128
    bins = BAND_FIRST_BIN + order
    cos, sin = phase(bins[:, None] * np.arange(LAG_NEAR)[None, :])
    table = np.concatenate([cos, -sin], axis=0) * scale
    far = np.arange(LAGS // LAG_NEAR) * LAG_NEAR - LAGS // 2
    turn = phase(far[:, None] * bins[None, :])
    return split(table), np.stack(turn).astype(np.float32)


def halves(value):
    high = value.astype(BF16)
    return high, (value - high.astype(F32)).astype(BF16)


def zigzag(step):
    return 4 + (step + 1) // 2 * (1 - 2 * (step % 2))


def kernel(
    chans, windows,
    x_hbm, map_hbm, pairs_hbm, count_hbm, fwd_hbm, fturn_hbm, inv_hbm, iturn_hbm,
    out_ref,
    x_ref, map_ref, pairs_ref, count_ref, fwd_ref, fturn_ref, inv_ref, iturn_ref,
    even_h, even_l, odd_h, odd_l, zr_ref, zi_ref, spec_ref,
    g_ref, r1_ref, wide_ref, s_ref, r2_ref, h_ref, sel_ref, m_ref, q_ref, m2_ref, u_ref, lag_h, lag_l,
    load_sem, send_sem, recv_sem,
):
    c, t = lax.axis_index("chan"), lax.axis_index("tm")
    rows, samples = x_ref.shape
    sections = samples // NEAR
    ends = [
        (x_hbm, x_ref), (fwd_hbm, fwd_ref), (fturn_hbm, fturn_ref), (map_hbm, map_ref),
        (pairs_hbm, pairs_ref), (count_hbm, count_ref), (iturn_hbm, iturn_ref), (inv_hbm, inv_ref),
    ]
    loads = [
        pltpu.make_async_copy(source, target, load_sem.at[k]) for k, (source, target) in enumerate(ends)
    ]
    def window_peer(step):
        z = lax.rem(t // 8 + zigzag(step[0]), 8)
        y = lax.rem(lax.rem(t, 8) + zigzag(step[1]), 8)
        return z * 8 + y

    def diagonal(total, action):
        @pl.loop(max(0, total - 7), min(7, total) + 1)
        def _(i):
            action((i, total - i))

    barrier = pltpu.get_barrier_semaphore()

    def greet(step):
        pl.semaphore_signal(barrier, 1, device_id=(c, window_peer(step)), device_id_type=MESH)

    for total in range(7):
        diagonal(total, greet)
    for load in loads[:6]:
        load.start()
    for total in range(7, 14):
        diagonal(total, greet)

    @pl.loop(1, chans)
    def _(step):
        pl.semaphore_signal(barrier, 1, device_id=(lax.rem(c + step, chans), t), device_id_type=MESH)

    half = NEAR // 2
    mirror = (
        lax.broadcasted_iota(jnp.int32, (half, half), 0) + lax.broadcasted_iota(jnp.int32, (half, half), 1)
        == half - 1
    ).astype(F32).astype(BF16)
    loads[0].wait()
    for b in range(sections):
        place = slice(b * rows, (b + 1) * rows)
        even_h[place, :], even_l[place, :] = halves(x_ref[:, b * NEAR : b * NEAR + half])
    back = jnp.dot(even_h[...], mirror, preferred_element_type=F32) + jnp.dot(
        even_l[...], mirror, preferred_element_type=F32
    )
    for b in range(sections):
        place = slice(b * rows, (b + 1) * rows)
        ahead = x_ref[:, b * NEAR + half : (b + 1) * NEAR]
        even_h[place, :], even_l[place, :] = halves(ahead + back[place])
        odd_h[place, :], odd_l[place, :] = halves(ahead - back[place])
    loads[1].wait()
    loads[2].wait()
    for load in loads[6:]:
        load.start()

    def product(high, low, part, lanes):
        return (
            jnp.dot(high[...], fwd_ref[0, part, :, lanes], preferred_element_type=F32)
            + jnp.dot(low[...], fwd_ref[0, part, :, lanes], preferred_element_type=F32)
            + jnp.dot(high[...], fwd_ref[1, part, :, lanes], preferred_element_type=F32)
        )

    for n in range(BINS // half):
        lanes = slice(half * n, half * (n + 1))
        zr_ref[...] = product(even_h, even_l, 0, lanes)
        zi_ref[...] = product(odd_h, odd_l, 1, lanes)
        re = jnp.zeros((rows, half), F32)
        im = jnp.zeros((rows, half), F32)
        for b in range(sections):
            zr = zr_ref[b * rows : (b + 1) * rows, :]
            zi = zi_ref[b * rows : (b + 1) * rows, :]
            cw = fturn_ref[0, b : b + 1, lanes]
            sw = fturn_ref[1, b : b + 1, lanes]
            re += zr * cw + zi * sw
            im += zi * cw - zr * sw
        spec_ref[:rows, lanes] = re
        spec_ref[rows:, lanes] = im

    re, im = spec_ref[:rows, :], spec_ref[rows:, :]
    power = re * re + im * im
    level = jnp.mean(power, axis=1, keepdims=True)
    inverse = 1.0 / jnp.sqrt(power + level + 1e-06)
    white = jnp.concatenate([re * inverse, im * inverse], axis=0).astype(BF16)

    loads[3].wait()
    place = jnp.bitwise_and(map_ref[...], rows - 1).reshape(1, rows)
    place = jnp.concatenate([place, place + rows], axis=1)
    pick = (lax.broadcasted_iota(jnp.int32, (2 * rows, 2 * rows), 0) == place).astype(F32).astype(BF16)
    g = lax.dot_general(white, pick, (((0,), (0,)), ((), ())), preferred_element_type=F32)
    g_ref[...] = g.reshape(windows, chans, 2 * rows).astype(BF16)

    pl.semaphore_wait(barrier, windows + chans - 2)

    def send_window(source, target, k):
        def action(step):
            peer = window_peer(step)
            pltpu.make_async_remote_copy(
                src_ref=source.at[peer], dst_ref=target.at[t], send_sem=send_sem.at[k],
                recv_sem=recv_sem.at[k], device_id=(c, peer), device_id_type=MESH,
            ).start()

        for total in range(14):
            diagonal(total, action)
        target[t] = source[t]

    def arrived(ref, k):
        rest = ref.at[pl.ds(0, ref.shape[0] - 1)]
        pltpu.make_async_copy(rest, rest, recv_sem.at[k]).wait()

    def sent(ref, k):
        rest = ref.at[pl.ds(0, ref.shape[0] - 1)]
        pltpu.make_async_copy(rest, rest, send_sem.at[k]).wait()

    send_window(g_ref, r1_ref, 0)

    for load in loads[4:]:
        load.wait()
    gap = lax.broadcasted_iota(jnp.int32, (BLOCK, chans * rows), 1) - lax.broadcasted_iota(
        jnp.int32, (BLOCK, chans * rows), 0
    )
    wide = SLOTS * BLOCK
    owners = [lax.rem(c + zigzag(step) % chans, chans) for step in range(chans)]
    for step in range(chans):
        for side in range(2):
            for s in range(SLOTS):
                hit = gap == pairs_ref[side, owners[step] * SLOTS + s] * BLOCK
                first = (step * 2 + side) * wide + s * BLOCK
                sel_ref[first : first + BLOCK, :] = hit.astype(F32).astype(BF16)
    arrived(r1_ref, 0)
    wide_ref[...] = r1_ref[...].astype(F32)
    for q in range(chans):
        s_ref[q] = wide_ref[:, q, :].astype(BF16)

    @pl.loop(0, chans - 1)
    def _(step):
        peer = lax.rem(c + zigzag(step), chans)
        pltpu.make_async_remote_copy(
            src_ref=s_ref.at[peer], dst_ref=r2_ref.at[c], send_sem=send_sem.at[1],
            recv_sem=recv_sem.at[1], device_id=(peer, t), device_id_type=MESH,
        ).start()

    r2_ref[c] = s_ref[c]
    arrived(r2_ref, 1)

    for d in range(0, chans, 2):
        one = r2_ref[d].astype(F32)
        two = r2_ref[d + 1].astype(F32)
        first = lax.broadcasted_iota(jnp.int32, one.shape, 1) < rows
        re = jnp.where(first, one, pltpu.roll(two, rows, 1))
        im = jnp.where(first, pltpu.roll(one, rows, 1), two)
        value = jnp.concatenate([re, im, -im, re], axis=0)
        h_ref[:, d * rows : (d + 2) * rows] = value.astype(BF16)
    pick = lax.dot_general(
        sel_ref[...], h_ref[...], (((1,), (1,)), ((), ())), preferred_element_type=F32
    ).astype(BF16)

    same = (
        lax.broadcasted_iota(jnp.int32, (wide, LANES), 0) // BLOCK
        == lax.broadcasted_iota(jnp.int32, (wide, LANES), 1) // (2 * BLOCK)
    )

    def owner_pairs(step):
        left = pick[2 * step * wide : (2 * step + 1) * wide, :LANES]
        both = pick[(2 * step + 1) * wide : (2 * step + 2) * wide]
        right = []
        for s in range(SLOTS):
            right += [both[s * BLOCK : (s + 1) * BLOCK, :LANES], both[s * BLOCK : (s + 1) * BLOCK, LANES:]]
        right = jnp.concatenate(right, axis=0)
        cross = lax.dot_general(left, right, (((1,), (1,)), ((), ())), preferred_element_type=F32)
        cross = jnp.where(same, cross, 0.0)
        return sum(cross[s * BLOCK : (s + 1) * BLOCK] for s in range(SLOTS))

    for step in range(chans - 1):
        m_ref[step] = owner_pairs(step)
        pltpu.make_async_remote_copy(
            src_ref=m_ref.at[step], dst_ref=q_ref.at[c], send_sem=send_sem.at[2],
            recv_sem=recv_sem.at[2], device_id=(owners[step], t), device_id_type=MESH,
        ).start()
    q_ref[c] = owner_pairs(chans - 1)
    arrived(q_ref, 2)

    block = lax.broadcasted_iota(jnp.int32, (BLOCK, LANES), 1) // (2 * BLOCK)
    for s in range(SLOTS):
        for h in range(2):
            mixed = jnp.zeros((BLOCK, LANES), F32)
            for k in range(4):
                part = q_ref[4 * h + k]
                shift = (k - s) * 2 * BLOCK % LANES
                part = pltpu.roll(part, shift, 1) if shift else part
                mixed = jnp.where(block == k, part, mixed)
            m2_ref[s * BLOCK : (s + 1) * BLOCK, h, :] = mixed
    send_window(m2_ref, u_ref, 3)
    arrived(u_ref, 3)

    turned = jnp.concatenate([u_ref[:, 0, :], u_ref[:, 1, :]], axis=0).T
    row_ids = t * BLOCK + lax.broadcasted_iota(jnp.int32, (BLOCK, 1), 0)
    live = (row_ids < count_ref[c]).astype(F32)
    re = jnp.concatenate([turned[32 * k : 32 * k + 16] for k in range(4)], axis=1) * live
    im = jnp.concatenate([turned[32 * k + 16 : 32 * k + 32] for k in range(4)], axis=1) * live
    for n in range(LAGS // LAG_NEAR):
        cw, sw = iturn_ref[0, n : n + 1, :], iturn_ref[1, n : n + 1, :]
        place = slice(n * BLOCK, (n + 1) * BLOCK)
        high, low = halves(re * cw - im * sw)
        lag_h[place, :BINS] = high
        lag_l[place, :BINS] = low
        high, low = halves(re * sw + im * cw)
        lag_h[place, BINS:] = high
        lag_l[place, BINS:] = low
    lags = (
        jnp.dot(lag_h[...], inv_ref[0], preferred_element_type=F32)
        + jnp.dot(lag_l[...], inv_ref[0], preferred_element_type=F32)
        + jnp.dot(lag_h[...], inv_ref[1], preferred_element_type=F32)
    )
    for n in range(LAGS // LAG_NEAR):
        out_ref[:, n * LAG_NEAR : (n + 1) * LAG_NEAR] = lags[n * BLOCK : (n + 1) * BLOCK]
    sent(g_ref, 0)
    sent(s_ref, 1)
    sent(m_ref, 2)
    sent(m2_ref, 3)


def solution(mesh):
    chans, windows = mesh.shape["chan"], mesh.shape["tm"]

    def body(traces, channel_map, pair_blocks, pair_count):
        _, rows, samples = traces.shape
        fwd, fturn = forward_tables(samples)
        inv, iturn = inverse_tables(1.0 / math.sqrt(windows * BINS))
        sections, far = samples // NEAR, LAGS // LAG_NEAR
        vmem = pl.BlockSpec(memory_space=pltpu.VMEM)
        hbm = pl.BlockSpec(memory_space=pltpu.HBM)
        return pl.pallas_call(
            functools.partial(kernel, chans, windows),
            out_shape=pltpu.VMEM((BLOCK, LAGS), F32),
            in_specs=[hbm] * 8,
            out_specs=vmem,
            scratch_shapes=[
                pltpu.VMEM((rows, samples), F32),
                pltpu.VMEM(channel_map.shape, jnp.int32),
                pltpu.SMEM(pair_blocks.shape[::-1], jnp.int32),
                pltpu.SMEM(pair_count.shape, jnp.int32),
                pltpu.VMEM(fwd.shape, BF16),
                pltpu.VMEM(fturn.shape, F32),
                pltpu.VMEM(inv.shape, BF16),
                pltpu.VMEM(iturn.shape, F32),
                pltpu.VMEM((sections * rows, NEAR // 2), BF16),
                pltpu.VMEM((sections * rows, NEAR // 2), BF16),
                pltpu.VMEM((sections * rows, NEAR // 2), BF16),
                pltpu.VMEM((sections * rows, NEAR // 2), BF16),
                pltpu.VMEM((sections * rows, NEAR // 2), F32),
                pltpu.VMEM((sections * rows, NEAR // 2), F32),
                pltpu.VMEM((2 * rows, BINS), F32),
                pltpu.VMEM((windows, chans, 2 * rows), BF16),
                pltpu.VMEM((windows, chans, 2 * rows), BF16),
                pltpu.VMEM((windows, chans, 2 * rows), F32),
                pltpu.VMEM((chans, windows, 2 * rows), BF16),
                pltpu.VMEM((chans, windows, 2 * rows), BF16),
                pltpu.VMEM((4 * windows, chans * rows), BF16),
                pltpu.VMEM((2 * pair_blocks.shape[0] * BLOCK, chans * rows), BF16),
                pltpu.VMEM((chans, BLOCK, LANES), F32),
                pltpu.VMEM((chans, BLOCK, LANES), F32),
                pltpu.VMEM((windows, 2, LANES), F32),
                pltpu.VMEM((windows, 2, LANES), F32),
                pltpu.VMEM((far * BLOCK, 2 * BINS), BF16),
                pltpu.VMEM((far * BLOCK, 2 * BINS), BF16),
                pltpu.SemaphoreType.DMA((8,)),
                pltpu.SemaphoreType.DMA((4,)),
                pltpu.SemaphoreType.DMA((4,)),
            ],
            compiler_params=pltpu.CompilerParams(
                collective_id=0, has_side_effects=True, vmem_limit_bytes=56 << 20
            ),
            name="correlate",
        )(traces[0], channel_map, pair_blocks.T, pair_count, fwd, fturn, inv, iturn)

    placed = (P("tm", "chan", None), P("chan"), P(), P())
    return jax.shard_map(
        body, mesh=mesh, in_specs=placed, out_specs=P(("chan", "tm"), None), check_vma=False
    )
```

```python
import functools
import math

import jax
import jax.numpy as jnp
import numpy as np
from jax import lax
from jax.experimental import pallas as pl
from jax.experimental.pallas import tpu as pltpu
from jax.sharding import PartitionSpec as P

BLOCK = 16
SLOTS = 4
TRANSFORM_LENGTH = 16384
BAND_FIRST_BIN = 80
BINS = 512
LAGS = 4096
NEAR = 512
LAG_NEAR = 512
LANES = 128
MESH = pl.DeviceIdType.MESH
F32 = jnp.float32
BF16 = jnp.bfloat16


def phase(products, length=TRANSFORM_LENGTH):
    angles = np.mod(products, length) * (2.0 * math.pi / length)
    return np.cos(angles), np.sin(angles)


def split(table):
    table = table.astype(np.float32)
    high = table.astype(BF16)
    low = (table - high.astype(np.float32)).astype(BF16)
    return np.stack([high, low])


def forward_tables(samples):
    bins = BAND_FIRST_BIN + np.arange(BINS)
    offset = 2 * np.arange(NEAR // 2) + 1
    cos, sin = phase(offset[:, None] * bins[None, :], 2 * TRANSFORM_LENGTH)
    centre = 2 * NEAR * np.arange(samples // NEAR) + NEAR - 1
    turn = phase(centre[:, None] * bins[None, :], 2 * TRANSFORM_LENGTH)
    return split(np.stack([cos, -sin])), np.stack(turn).astype(np.float32)


def inverse_tables(scale):
    lane = np.arange(BINS)
    order = 8 * (lane % 64) + 4 * (lane // 64 % 2) + lane // 128
    bins = BAND_FIRST_BIN + order
    cos, sin = phase(bins[:, None] * np.arange(LAG_NEAR)[None, :])
    table = np.concatenate([cos, -sin], axis=0) * scale
    far = np.arange(LAGS // LAG_NEAR) * LAG_NEAR - LAGS // 2
    turn = phase(far[:, None] * bins[None, :])
    return split(table), np.stack(turn).astype(np.float32)


def halves(value):
    high = value.astype(BF16)
    return high, (value - high.astype(F32)).astype(BF16)


def zigzag(step):
    return 4 + (step + 1) // 2 * (1 - 2 * (step % 2))


def kernel(
    chans, windows,
    x_hbm, map_hbm, pairs_hbm, count_hbm, fwd_hbm, fturn_hbm, inv_hbm, iturn_hbm,
    out_ref,
    x_ref, map_ref, pairs_ref, count_ref, fwd_ref, fturn_ref, inv_ref, iturn_ref,
    even_h, even_l, odd_h, odd_l, zr_ref, zi_ref, spec_ref,
    g_ref, r1_ref, wide_ref, s_ref, r2_ref, h_ref, sel_ref, m_ref, q_ref, m2_ref, u_ref, lag_h, lag_l,
    load_sem, send_sem, recv_sem,
):
    c, t = lax.axis_index("chan"), lax.axis_index("tm")
    rows, samples = x_ref.shape
    sections = samples // NEAR
    ends = [
        (x_hbm, x_ref), (fwd_hbm, fwd_ref), (fturn_hbm, fturn_ref), (map_hbm, map_ref),
        (pairs_hbm, pairs_ref), (count_hbm, count_ref), (iturn_hbm, iturn_ref), (inv_hbm, inv_ref),
    ]
    loads = [
        pltpu.make_async_copy(source, target, load_sem.at[k]) for k, (source, target) in enumerate(ends)
    ]
    def window_peer(step):
        z = lax.rem(t // 8 + zigzag(step[0]), 8)
        y = lax.rem(lax.rem(t, 8) + zigzag(step[1]), 8)
        return z * 8 + y

    def diagonal(total, action):
        for i in range(max(0, total - 7), min(7, total) + 1):
            action((i, total - i))

    barrier = pltpu.get_barrier_semaphore()

    def greet(step):
        pl.semaphore_signal(barrier, 1, device_id=(c, window_peer(step)), device_id_type=MESH)

    for total in range(7):
        diagonal(total, greet)
    for load in loads[:6]:
        load.start()
    for total in range(7, 14):
        diagonal(total, greet)

    @pl.loop(1, chans)
    def _(step):
        pl.semaphore_signal(barrier, 1, device_id=(lax.rem(c + step, chans), t), device_id_type=MESH)

    half = NEAR // 2
    mirror = (
        lax.broadcasted_iota(jnp.int32, (half, half), 0) + lax.broadcasted_iota(jnp.int32, (half, half), 1)
        == half - 1
    ).astype(F32).astype(BF16)
    loads[0].wait()
    for b in range(sections):
        place = slice(b * rows, (b + 1) * rows)
        even_h[place, :], even_l[place, :] = halves(x_ref[:, b * NEAR : b * NEAR + half])
    back = jnp.dot(even_h[...], mirror, preferred_element_type=F32) + jnp.dot(
        even_l[...], mirror, preferred_element_type=F32
    )
    for b in range(sections):
        place = slice(b * rows, (b + 1) * rows)
        ahead = x_ref[:, b * NEAR + half : (b + 1) * NEAR]
        even_h[place, :], even_l[place, :] = halves(ahead + back[place])
        odd_h[place, :], odd_l[place, :] = halves(ahead - back[place])
    loads[1].wait()
    loads[2].wait()
    for load in loads[6:]:
        load.start()

    def product(high, low, part, lanes):
        return (
            jnp.dot(high[...], fwd_ref[0, part, :, lanes], preferred_element_type=F32)
            + jnp.dot(low[...], fwd_ref[0, part, :, lanes], preferred_element_type=F32)
            + jnp.dot(high[...], fwd_ref[1, part, :, lanes], preferred_element_type=F32)
        )

    for n in range(BINS // half):
        lanes = slice(half * n, half * (n + 1))
        zr_ref[...] = product(even_h, even_l, 0, lanes)
        zi_ref[...] = product(odd_h, odd_l, 1, lanes)
        re = jnp.zeros((rows, half), F32)
        im = jnp.zeros((rows, half), F32)
        for b in range(sections):
            zr = zr_ref[b * rows : (b + 1) * rows, :]
            zi = zi_ref[b * rows : (b + 1) * rows, :]
            cw = fturn_ref[0, b : b + 1, lanes]
            sw = fturn_ref[1, b : b + 1, lanes]
            re += zr * cw + zi * sw
            im += zi * cw - zr * sw
        spec_ref[:rows, lanes] = re
        spec_ref[rows:, lanes] = im

    re, im = spec_ref[:rows, :], spec_ref[rows:, :]
    power = re * re + im * im
    level = jnp.mean(power, axis=1, keepdims=True)
    inverse = 1.0 / jnp.sqrt(power + level + 1e-06)
    white = jnp.concatenate([re * inverse, im * inverse], axis=0).astype(BF16)

    loads[3].wait()
    place = jnp.bitwise_and(map_ref[...], rows - 1).reshape(1, rows)
    place = jnp.concatenate([place, place + rows], axis=1)
    pick = (lax.broadcasted_iota(jnp.int32, (2 * rows, 2 * rows), 0) == place).astype(F32).astype(BF16)
    g = lax.dot_general(white, pick, (((0,), (0,)), ((), ())), preferred_element_type=F32)
    g_ref[...] = g.reshape(windows, chans, 2 * rows).astype(BF16)

    pl.semaphore_wait(barrier, windows + chans - 2)

    def send_window(source, target, k):
        def action(step):
            peer = window_peer(step)
            pltpu.make_async_remote_copy(
                src_ref=source.at[peer], dst_ref=target.at[t], send_sem=send_sem.at[k],
                recv_sem=recv_sem.at[k], device_id=(c, peer), device_id_type=MESH,
            ).start()

        for total in range(14):
            diagonal(total, action)
        target[t] = source[t]

    def arrived(ref, k):
        rest = ref.at[pl.ds(0, ref.shape[0] - 1)]
        pltpu.make_async_copy(rest, rest, recv_sem.at[k]).wait()

    def sent(ref, k):
        rest = ref.at[pl.ds(0, ref.shape[0] - 1)]
        pltpu.make_async_copy(rest, rest, send_sem.at[k]).wait()

    send_window(g_ref, r1_ref, 0)

    for load in loads[4:]:
        load.wait()
    gap = lax.broadcasted_iota(jnp.int32, (BLOCK, chans * rows), 1) - lax.broadcasted_iota(
        jnp.int32, (BLOCK, chans * rows), 0
    )
    wide = SLOTS * BLOCK
    owners = [lax.rem(c + zigzag(step) % chans, chans) for step in range(chans)]
    for step in range(chans):
        for side in range(2):
            for s in range(SLOTS):
                hit = gap == pairs_ref[side, owners[step] * SLOTS + s] * BLOCK
                first = (step * 2 + side) * wide + s * BLOCK
                sel_ref[first : first + BLOCK, :] = hit.astype(F32).astype(BF16)
    arrived(r1_ref, 0)
    wide_ref[...] = r1_ref[...].astype(F32)
    for q in range(chans):
        s_ref[q] = wide_ref[:, q, :].astype(BF16)

    @pl.loop(0, chans - 1, unroll=True)
    def _(step):
        peer = lax.rem(c + zigzag(step), chans)
        pltpu.make_async_remote_copy(
            src_ref=s_ref.at[peer], dst_ref=r2_ref.at[c], send_sem=send_sem.at[1],
            recv_sem=recv_sem.at[1], device_id=(peer, t), device_id_type=MESH,
        ).start()

    r2_ref[c] = s_ref[c]
    arrived(r2_ref, 1)

    for d in range(0, chans, 2):
        one = r2_ref[d].astype(F32)
        two = r2_ref[d + 1].astype(F32)
        first = lax.broadcasted_iota(jnp.int32, one.shape, 1) < rows
        re = jnp.where(first, one, pltpu.roll(two, rows, 1))
        im = jnp.where(first, pltpu.roll(one, rows, 1), two)
        value = jnp.concatenate([re, im, -im, re], axis=0)
        h_ref[:, d * rows : (d + 2) * rows] = value.astype(BF16)
    pick = lax.dot_general(
        sel_ref[...], h_ref[...], (((1,), (1,)), ((), ())), preferred_element_type=F32
    ).astype(BF16)

    same = (
        lax.broadcasted_iota(jnp.int32, (wide, LANES), 0) // BLOCK
        == lax.broadcasted_iota(jnp.int32, (wide, LANES), 1) // (2 * BLOCK)
    )

    def owner_pairs(step):
        left = pick[2 * step * wide : (2 * step + 1) * wide, :LANES]
        both = pick[(2 * step + 1) * wide : (2 * step + 2) * wide]
        right = []
        for s in range(SLOTS):
            right += [both[s * BLOCK : (s + 1) * BLOCK, :LANES], both[s * BLOCK : (s + 1) * BLOCK, LANES:]]
        right = jnp.concatenate(right, axis=0)
        cross = lax.dot_general(left, right, (((1,), (1,)), ((), ())), preferred_element_type=F32)
        cross = jnp.where(same, cross, 0.0)
        return sum(cross[s * BLOCK : (s + 1) * BLOCK] for s in range(SLOTS))

    for step in range(chans - 1):
        m_ref[step] = owner_pairs(step)
        pltpu.make_async_remote_copy(
            src_ref=m_ref.at[step], dst_ref=q_ref.at[c], send_sem=send_sem.at[2],
            recv_sem=recv_sem.at[2], device_id=(owners[step], t), device_id_type=MESH,
        ).start()
    q_ref[c] = owner_pairs(chans - 1)
    arrived(q_ref, 2)

    block = lax.broadcasted_iota(jnp.int32, (BLOCK, LANES), 1) // (2 * BLOCK)
    for s in range(SLOTS):
        for h in range(2):
            mixed = jnp.zeros((BLOCK, LANES), F32)
            for k in range(4):
                part = q_ref[4 * h + k]
                shift = (k - s) * 2 * BLOCK % LANES
                part = pltpu.roll(part, shift, 1) if shift else part
                mixed = jnp.where(block == k, part, mixed)
            m2_ref[s * BLOCK : (s + 1) * BLOCK, h, :] = mixed
    send_window(m2_ref, u_ref, 3)
    arrived(u_ref, 3)

    turned = jnp.concatenate([u_ref[:, 0, :], u_ref[:, 1, :]], axis=0).T
    row_ids = t * BLOCK + lax.broadcasted_iota(jnp.int32, (BLOCK, 1), 0)
    live = (row_ids < count_ref[c]).astype(F32)
    re = jnp.concatenate([turned[32 * k : 32 * k + 16] for k in range(4)], axis=1) * live
    im = jnp.concatenate([turned[32 * k + 16 : 32 * k + 32] for k in range(4)], axis=1) * live
    for n in range(LAGS // LAG_NEAR):
        cw, sw = iturn_ref[0, n : n + 1, :], iturn_ref[1, n : n + 1, :]
        place = slice(n * BLOCK, (n + 1) * BLOCK)
        high, low = halves(re * cw - im * sw)
        lag_h[place, :BINS] = high
        lag_l[place, :BINS] = low
        high, low = halves(re * sw + im * cw)
        lag_h[place, BINS:] = high
        lag_l[place, BINS:] = low
    lags = (
        jnp.dot(lag_h[...], inv_ref[0], preferred_element_type=F32)
        + jnp.dot(lag_l[...], inv_ref[0], preferred_element_type=F32)
        + jnp.dot(lag_h[...], inv_ref[1], preferred_element_type=F32)
    )
    for n in range(LAGS // LAG_NEAR):
        out_ref[:, n * LAG_NEAR : (n + 1) * LAG_NEAR] = lags[n * BLOCK : (n + 1) * BLOCK]
    sent(g_ref, 0)
    sent(s_ref, 1)
    sent(m_ref, 2)
    sent(m2_ref, 3)


def solution(mesh):
    chans, windows = mesh.shape["chan"], mesh.shape["tm"]

    def body(traces, channel_map, pair_blocks, pair_count):
        _, rows, samples = traces.shape
        fwd, fturn = forward_tables(samples)
        inv, iturn = inverse_tables(1.0 / math.sqrt(windows * BINS))
        sections, far = samples // NEAR, LAGS // LAG_NEAR
        vmem = pl.BlockSpec(memory_space=pltpu.VMEM)
        hbm = pl.BlockSpec(memory_space=pltpu.HBM)
        return pl.pallas_call(
            functools.partial(kernel, chans, windows),
            out_shape=pltpu.VMEM((BLOCK, LAGS), F32),
            in_specs=[hbm] * 8,
            out_specs=vmem,
            scratch_shapes=[
                pltpu.VMEM((rows, samples), F32),
                pltpu.VMEM(channel_map.shape, jnp.int32),
                pltpu.SMEM(pair_blocks.shape[::-1], jnp.int32),
                pltpu.SMEM(pair_count.shape, jnp.int32),
                pltpu.VMEM(fwd.shape, BF16),
                pltpu.VMEM(fturn.shape, F32),
                pltpu.VMEM(inv.shape, BF16),
                pltpu.VMEM(iturn.shape, F32),
                pltpu.VMEM((sections * rows, NEAR // 2), BF16),
                pltpu.VMEM((sections * rows, NEAR // 2), BF16),
                pltpu.VMEM((sections * rows, NEAR // 2), BF16),
                pltpu.VMEM((sections * rows, NEAR // 2), BF16),
                pltpu.VMEM((sections * rows, NEAR // 2), F32),
                pltpu.VMEM((sections * rows, NEAR // 2), F32),
                pltpu.VMEM((2 * rows, BINS), F32),
                pltpu.VMEM((windows, chans, 2 * rows), BF16),
                pltpu.VMEM((windows, chans, 2 * rows), BF16),
                pltpu.VMEM((windows, chans, 2 * rows), F32),
                pltpu.VMEM((chans, windows, 2 * rows), BF16),
                pltpu.VMEM((chans, windows, 2 * rows), BF16),
                pltpu.VMEM((4 * windows, chans * rows), BF16),
                pltpu.VMEM((2 * pair_blocks.shape[0] * BLOCK, chans * rows), BF16),
                pltpu.VMEM((chans, BLOCK, LANES), F32),
                pltpu.VMEM((chans, BLOCK, LANES), F32),
                pltpu.VMEM((windows, 2, LANES), F32),
                pltpu.VMEM((windows, 2, LANES), F32),
                pltpu.VMEM((far * BLOCK, 2 * BINS), BF16),
                pltpu.VMEM((far * BLOCK, 2 * BINS), BF16),
                pltpu.SemaphoreType.DMA((8,)),
                pltpu.SemaphoreType.DMA((4,)),
                pltpu.SemaphoreType.DMA((4,)),
            ],
            compiler_params=pltpu.CompilerParams(
                collective_id=0, has_side_effects=True, vmem_limit_bytes=56 << 20
            ),
            name="correlate",
        )(traces[0], channel_map, pair_blocks.T, pair_count, fwd, fturn, inv, iturn)

    placed = (P("tm", "chan", None), P("chan"), P(), P())
    return jax.shard_map(
        body, mesh=mesh, in_specs=placed, out_specs=P(("chan", "tm"), None), check_vma=False
    )
```

```python
import functools
import math

import jax
import jax.numpy as jnp
import numpy as np
from jax import lax
from jax.experimental import pallas as pl
from jax.experimental.pallas import tpu as pltpu
from jax.sharding import PartitionSpec as P

BLOCK = 16
SLOTS = 4
TRANSFORM_LENGTH = 16384
BAND_FIRST_BIN = 80
BINS = 512
LAGS = 4096
NEAR = 512
LAG_NEAR = 512
LANES = 128
MESH = pl.DeviceIdType.MESH
F32 = jnp.float32
BF16 = jnp.bfloat16


def phase(products, length=TRANSFORM_LENGTH):
    angles = np.mod(products, length) * (2.0 * math.pi / length)
    return np.cos(angles), np.sin(angles)


def split(table):
    table = table.astype(np.float32)
    high = table.astype(BF16)
    low = (table - high.astype(np.float32)).astype(BF16)
    return np.stack([high, low])


def forward_tables(samples):
    bins = BAND_FIRST_BIN + np.arange(BINS)
    offset = 2 * np.arange(NEAR // 2) + 1
    cos, sin = phase(offset[:, None] * bins[None, :], 2 * TRANSFORM_LENGTH)
    centre = 2 * NEAR * np.arange(samples // NEAR) + NEAR - 1
    turn = phase(centre[:, None] * bins[None, :], 2 * TRANSFORM_LENGTH)
    return split(np.stack([cos, -sin])), np.stack(turn).astype(np.float32)


def inverse_tables(scale):
    lane = np.arange(BINS)
    order = 8 * (lane % 64) + 4 * (lane // 64 % 2) + lane // 128
    bins = BAND_FIRST_BIN + order
    cos, sin = phase(bins[:, None] * np.arange(LAG_NEAR)[None, :])
    table = np.concatenate([cos, -sin], axis=0) * scale
    far = np.arange(LAGS // LAG_NEAR) * LAG_NEAR - LAGS // 2
    turn = phase(far[:, None] * bins[None, :])
    return split(table), np.stack(turn).astype(np.float32)


def halves(value):
    high = value.astype(BF16)
    return high, (value - high.astype(F32)).astype(BF16)


def zigzag(step):
    return 4 + (step + 1) // 2 * (1 - 2 * (step % 2))


def kernel(
    chans, windows,
    x_hbm, map_hbm, pairs_hbm, count_hbm, fwd_hbm, fturn_hbm, inv_hbm, iturn_hbm,
    out_ref,
    x_ref, map_ref, pairs_ref, count_ref, fwd_ref, fturn_ref, inv_ref, iturn_ref,
    even_h, even_l, odd_h, odd_l, zr_ref, zi_ref, spec_ref,
    g_ref, r1_ref, wide_ref, s_ref, r2_ref, h_ref, sel_ref, m_ref, q_ref, m2_ref, u_ref, lag_ref,
    load_sem, send_sem, recv_sem,
):
    c, t = lax.axis_index("chan"), lax.axis_index("tm")
    rows, samples = x_ref.shape
    sections = samples // NEAR
    ends = [
        (x_hbm, x_ref), (fwd_hbm, fwd_ref), (fturn_hbm, fturn_ref), (map_hbm, map_ref),
        (pairs_hbm, pairs_ref), (count_hbm, count_ref), (iturn_hbm, iturn_ref), (inv_hbm, inv_ref),
    ]
    loads = [
        pltpu.make_async_copy(source, target, load_sem.at[k]) for k, (source, target) in enumerate(ends)
    ]
    def window_peer(step):
        z = lax.rem(t // 8 + zigzag(step[0]), 8)
        y = lax.rem(lax.rem(t, 8) + zigzag(step[1]), 8)
        return z * 8 + y

    def diagonal(total, action):
        for i in range(max(0, total - 7), min(7, total) + 1):
            action((i, total - i))

    barrier = pltpu.get_barrier_semaphore()

    def greet(step):
        pl.semaphore_signal(barrier, 1, device_id=(c, window_peer(step)), device_id_type=MESH)

    for total in range(7):
        diagonal(total, greet)
    for load in loads[:6]:
        load.start()
    for total in range(7, 14):
        diagonal(total, greet)

    @pl.loop(1, chans)
    def _(step):
        pl.semaphore_signal(barrier, 1, device_id=(lax.rem(c + step, chans), t), device_id_type=MESH)

    half = NEAR // 2
    mirror = (
        lax.broadcasted_iota(jnp.int32, (half, half), 0) + lax.broadcasted_iota(jnp.int32, (half, half), 1)
        == half - 1
    ).astype(F32).astype(BF16)
    loads[0].wait()
    for b in range(sections):
        place = slice(b * rows, (b + 1) * rows)
        even_h[place, :], even_l[place, :] = halves(x_ref[:, b * NEAR : b * NEAR + half])
    back = jnp.dot(even_h[...], mirror, preferred_element_type=F32) + jnp.dot(
        even_l[...], mirror, preferred_element_type=F32
    )
    for b in range(sections):
        place = slice(b * rows, (b + 1) * rows)
        ahead = x_ref[:, b * NEAR + half : (b + 1) * NEAR]
        even_h[place, :], even_l[place, :] = halves(ahead + back[place])
        odd_h[place, :], odd_l[place, :] = halves(ahead - back[place])
    loads[1].wait()
    loads[2].wait()
    for load in loads[6:]:
        load.start()

    def product(high, low, part, lanes):
        return (
            jnp.dot(high[...], fwd_ref[0, part, :, lanes], preferred_element_type=F32)
            + jnp.dot(low[...], fwd_ref[0, part, :, lanes], preferred_element_type=F32)
            + jnp.dot(high[...], fwd_ref[1, part, :, lanes], preferred_element_type=F32)
        )

    for n in range(BINS // half):
        lanes = slice(half * n, half * (n + 1))
        zr_ref[...] = product(even_h, even_l, 0, lanes)
        zi_ref[...] = product(odd_h, odd_l, 1, lanes)
        re = jnp.zeros((rows, half), F32)
        im = jnp.zeros((rows, half), F32)
        for b in range(sections):
            zr = zr_ref[b * rows : (b + 1) * rows, :]
            zi = zi_ref[b * rows : (b + 1) * rows, :]
            cw = fturn_ref[0, b : b + 1, lanes]
            sw = fturn_ref[1, b : b + 1, lanes]
            re += zr * cw + zi * sw
            im += zi * cw - zr * sw
        spec_ref[:rows, lanes] = re
        spec_ref[rows:, lanes] = im

    re, im = spec_ref[:rows, :], spec_ref[rows:, :]
    power = re * re + im * im
    level = jnp.mean(power, axis=1, keepdims=True)
    inverse = 1.0 / jnp.sqrt(power + level + 1e-06)
    white = jnp.concatenate([re * inverse, im * inverse], axis=0).astype(BF16)

    loads[3].wait()
    place = jnp.bitwise_and(map_ref[...], rows - 1).reshape(1, rows)
    place = jnp.concatenate([place, place + rows], axis=1)
    pick = (lax.broadcasted_iota(jnp.int32, (2 * rows, 2 * rows), 0) == place).astype(F32).astype(BF16)
    g = lax.dot_general(white, pick, (((0,), (0,)), ((), ())), preferred_element_type=F32)
    g_ref[...] = g.reshape(windows, chans, 2 * rows).astype(BF16)

    pl.semaphore_wait(barrier, windows + chans - 2)

    def send_window(source, target, k):
        def action(step):
            peer = window_peer(step)
            pltpu.make_async_remote_copy(
                src_ref=source.at[peer], dst_ref=target.at[t], send_sem=send_sem.at[k],
                recv_sem=recv_sem.at[k], device_id=(c, peer), device_id_type=MESH,
            ).start()

        for total in range(14):
            diagonal(total, action)
        target[t] = source[t]

    def arrived(ref, k):
        rest = ref.at[pl.ds(0, ref.shape[0] - 1)]
        pltpu.make_async_copy(rest, rest, recv_sem.at[k]).wait()

    def sent(ref, k):
        rest = ref.at[pl.ds(0, ref.shape[0] - 1)]
        pltpu.make_async_copy(rest, rest, send_sem.at[k]).wait()

    send_window(g_ref, r1_ref, 0)

    for load in loads[4:]:
        load.wait()
    gap = lax.broadcasted_iota(jnp.int32, (BLOCK, chans * rows), 1) - lax.broadcasted_iota(
        jnp.int32, (BLOCK, chans * rows), 0
    )
    wide = SLOTS * BLOCK
    owners = [lax.rem(c + zigzag(step) % chans, chans) for step in range(chans)]
    for step in range(chans):
        for side in range(2):
            for s in range(SLOTS):
                hit = gap == pairs_ref[side, owners[step] * SLOTS + s] * BLOCK
                first = (step * 2 + side) * wide + s * BLOCK
                sel_ref[first : first + BLOCK, :] = hit.astype(F32).astype(BF16)
    arrived(r1_ref, 0)
    wide_ref[...] = r1_ref[...].astype(F32)
    for q in range(chans):
        s_ref[q] = wide_ref[:, q, :].astype(BF16)

    @pl.loop(0, chans - 1, unroll=True)
    def _(step):
        peer = lax.rem(c + zigzag(step), chans)
        pltpu.make_async_remote_copy(
            src_ref=s_ref.at[peer], dst_ref=r2_ref.at[c], send_sem=send_sem.at[1],
            recv_sem=recv_sem.at[1], device_id=(peer, t), device_id_type=MESH,
        ).start()

    r2_ref[c] = s_ref[c]
    arrived(r2_ref, 1)

    for d in range(0, chans, 2):
        one = r2_ref[d].astype(F32)
        two = r2_ref[d + 1].astype(F32)
        first = lax.broadcasted_iota(jnp.int32, one.shape, 1) < rows
        re = jnp.where(first, one, pltpu.roll(two, rows, 1))
        im = jnp.where(first, pltpu.roll(one, rows, 1), two)
        value = jnp.concatenate([re, im, -im, re], axis=0)
        h_ref[:, d * rows : (d + 2) * rows] = value.astype(BF16)
    pick = lax.dot_general(
        sel_ref[...], h_ref[...], (((1,), (1,)), ((), ())), preferred_element_type=F32
    ).astype(BF16)

    same = (
        lax.broadcasted_iota(jnp.int32, (wide, LANES), 0) // BLOCK
        == lax.broadcasted_iota(jnp.int32, (wide, LANES), 1) // (2 * BLOCK)
    )

    def owner_pairs(step):
        left = pick[2 * step * wide : (2 * step + 1) * wide, :LANES]
        both = pick[(2 * step + 1) * wide : (2 * step + 2) * wide]
        right = []
        for s in range(SLOTS):
            right += [both[s * BLOCK : (s + 1) * BLOCK, :LANES], both[s * BLOCK : (s + 1) * BLOCK, LANES:]]
        right = jnp.concatenate(right, axis=0)
        cross = lax.dot_general(left, right, (((1,), (1,)), ((), ())), preferred_element_type=F32)
        cross = jnp.where(same, cross, 0.0)
        return sum(cross[s * BLOCK : (s + 1) * BLOCK] for s in range(SLOTS))

    for step in range(chans - 1):
        m_ref[step] = owner_pairs(step)
        pltpu.make_async_remote_copy(
            src_ref=m_ref.at[step], dst_ref=q_ref.at[c], send_sem=send_sem.at[2],
            recv_sem=recv_sem.at[2], device_id=(owners[step], t), device_id_type=MESH,
        ).start()
    q_ref[c] = owner_pairs(chans - 1)
    arrived(q_ref, 2)

    block = lax.broadcasted_iota(jnp.int32, (BLOCK, LANES), 1) // (2 * BLOCK)
    for s in range(SLOTS):
        for h in range(2):
            mixed = jnp.zeros((BLOCK, LANES), F32)
            for k in range(4):
                part = q_ref[4 * h + k]
                shift = (k - s) * 2 * BLOCK % LANES
                part = pltpu.roll(part, shift, 1) if shift else part
                mixed = jnp.where(block == k, part, mixed)
            m2_ref[s * BLOCK : (s + 1) * BLOCK, h, :] = mixed
    send_window(m2_ref, u_ref, 3)
    arrived(u_ref, 3)

    turned = jnp.concatenate([u_ref[:, 0, :], u_ref[:, 1, :]], axis=0).T
    row_ids = t * BLOCK + lax.broadcasted_iota(jnp.int32, (BLOCK, 1), 0)
    live = (row_ids < count_ref[c]).astype(F32)
    re = jnp.concatenate([turned[32 * k : 32 * k + 16] for k in range(4)], axis=1) * live
    im = jnp.concatenate([turned[32 * k + 16 : 32 * k + 32] for k in range(4)], axis=1) * live
    depth = LAGS // LAG_NEAR * BLOCK
    for n in range(LAGS // LAG_NEAR):
        cw, sw = iturn_ref[0, n : n + 1, :], iturn_ref[1, n : n + 1, :]
        place, lower = slice(n * BLOCK, (n + 1) * BLOCK), slice(depth + n * BLOCK, depth + (n + 1) * BLOCK)
        lag_ref[place, :BINS], lag_ref[lower, :BINS] = halves(re * cw - im * sw)
        lag_ref[place, BINS:], lag_ref[lower, BINS:] = halves(re * sw + im * cw)
    both = jnp.dot(lag_ref[...], inv_ref[0], preferred_element_type=F32)
    lags = both[:depth] + both[depth:] + jnp.dot(lag_ref[:depth], inv_ref[1], preferred_element_type=F32)
    for n in range(LAGS // LAG_NEAR):
        out_ref[:, n * LAG_NEAR : (n + 1) * LAG_NEAR] = lags[n * BLOCK : (n + 1) * BLOCK]
    sent(g_ref, 0)
    sent(s_ref, 1)
    sent(m_ref, 2)
    sent(m2_ref, 3)


def solution(mesh):
    chans, windows = mesh.shape["chan"], mesh.shape["tm"]

    def body(traces, channel_map, pair_blocks, pair_count):
        _, rows, samples = traces.shape
        fwd, fturn = forward_tables(samples)
        inv, iturn = inverse_tables(1.0 / math.sqrt(windows * BINS))
        sections, far = samples // NEAR, LAGS // LAG_NEAR
        vmem = pl.BlockSpec(memory_space=pltpu.VMEM)
        hbm = pl.BlockSpec(memory_space=pltpu.HBM)
        return pl.pallas_call(
            functools.partial(kernel, chans, windows),
            out_shape=pltpu.VMEM((BLOCK, LAGS), F32),
            in_specs=[hbm] * 8,
            out_specs=vmem,
            scratch_shapes=[
                pltpu.VMEM((rows, samples), F32),
                pltpu.VMEM(channel_map.shape, jnp.int32),
                pltpu.SMEM(pair_blocks.shape[::-1], jnp.int32),
                pltpu.SMEM(pair_count.shape, jnp.int32),
                pltpu.VMEM(fwd.shape, BF16),
                pltpu.VMEM(fturn.shape, F32),
                pltpu.VMEM(inv.shape, BF16),
                pltpu.VMEM(iturn.shape, F32),
                pltpu.VMEM((sections * rows, NEAR // 2), BF16),
                pltpu.VMEM((sections * rows, NEAR // 2), BF16),
                pltpu.VMEM((sections * rows, NEAR // 2), BF16),
                pltpu.VMEM((sections * rows, NEAR // 2), BF16),
                pltpu.VMEM((sections * rows, NEAR // 2), F32),
                pltpu.VMEM((sections * rows, NEAR // 2), F32),
                pltpu.VMEM((2 * rows, BINS), F32),
                pltpu.VMEM((windows, chans, 2 * rows), BF16),
                pltpu.VMEM((windows, chans, 2 * rows), BF16),
                pltpu.VMEM((windows, chans, 2 * rows), F32),
                pltpu.VMEM((chans, windows, 2 * rows), BF16),
                pltpu.VMEM((chans, windows, 2 * rows), BF16),
                pltpu.VMEM((4 * windows, chans * rows), BF16),
                pltpu.VMEM((2 * pair_blocks.shape[0] * BLOCK, chans * rows), BF16),
                pltpu.VMEM((chans, BLOCK, LANES), F32),
                pltpu.VMEM((chans, BLOCK, LANES), F32),
                pltpu.VMEM((windows, 2, LANES), F32),
                pltpu.VMEM((windows, 2, LANES), F32),
                pltpu.VMEM((2 * far * BLOCK, 2 * BINS), BF16),
                pltpu.SemaphoreType.DMA((8,)),
                pltpu.SemaphoreType.DMA((4,)),
                pltpu.SemaphoreType.DMA((4,)),
            ],
            compiler_params=pltpu.CompilerParams(
                collective_id=0, has_side_effects=True, vmem_limit_bytes=56 << 20
            ),
            name="correlate",
        )(traces[0], channel_map, pair_blocks.T, pair_count, fwd, fturn, inv, iturn)

    placed = (P("tm", "chan", None), P("chan"), P(), P())
    return jax.shard_map(
        body, mesh=mesh, in_specs=placed, out_specs=P(("chan", "tm"), None), check_vma=False
    )
```
